32 devices in a mesh: tile: 8 (over z, x), lev: 4 (over y, core).
Axes of the slice: x: 2, y: 2, z: 4, core: 2. Of those that a mesh axis runs over, the one named last changes fastest.
Arguments:
- control_static: float32 [2, 128, 64, 128], P(None, 'lev', 'tile'), may hold values from -6 to 6
- control_ens: float32 [2, 128, 64, 128], P(None, 'lev', 'tile'), may hold values from -6 to 6
- ens_perts: bfloat16 [2, 2, 128, 64, 128], P(None, None, 'lev', 'tile'), may hold values from -2.5 to 2.5
- band_sqrt: float32 [8, 2, 128, 128], P('tile', None, 'lev'), may hold values from -1 to 2
- band_owner: int32 [8], replicated, may hold values from 0 to 7, each once
- scale_class: int32 [64, 128], P('tile'), may hold values from 0 to 7
- static_scales: float32 [8], replicated, may hold values from 0.5 to 4
- local_scales: float32 [8], replicated, may hold values from 1 to 8
- obs_source: int32 [4096, 1], P('tile'), may hold values from 0 to 7; in each aligned block of 512 rows (0 to 511, 512 to 1023, ...) at most 256 rows name the same one
- obs_column: int32 [4096], P('tile'), may hold values from 0 to 1023
- obs_jac: float32 [8, 128, 2, 128], P('tile', None, None, 'lev'), may hold values from -0.375 to 0.375
- innovation: float32 [128, 4096], P(None, 'tile'), may hold values from -6 to 6
- obs_weight: float32 [128, 4096], P(None, 'tile'), may hold values from 0.2 to 5
Outputs:
- analysis_increment: float32 [2, 128, 64, 128], P(None, 'lev', 'tile')
- final_static: float32 [2, 128, 64, 128], P(None, 'lev', 'tile')
- final_ens: float32 [2, 128, 64, 128], P(None, 'lev', 'tile')
The draws below stay inside these ranges and needn't reach their ends.
Inputs may be any that keep to these rules, and one draw needn't show every extreme that they name: `obs_source`: within each tile's block of 512 observations at most 256 name the same source tile, and some source tile is named exactly 256 times in some block. `band_owner`: each slot is named once.
All inputs are finite; a program needn't handle non-finite values.
Results may differ from the reference program's by a relative error of at most 0.0003.
Values sent between devices are 32-bit elements; how exact they have to be, the bound alone decides.
A program may use at most 64 MiB of HBM per device.

```python
import math
import jax
import jax.numpy as jnp
import numpy as np
from jax import lax

NVAR = 2
NLEV = 128
NCH = 128
NCLS = 8
NSWEEP = 4
ITERS = 2
LON_DEV = 8
LAT = 128
OBS_DEV = 512
ENS = 2
NLON = 64
NBAND = 8
CAP = 256
NOBS = 4096
N_TILE = 8


def draw_band_sqrt(key, part):
    first_key = jax.random.fold_in(key, 11)
    second_key = jax.random.fold_in(key, 23)
    shape_full = (NBAND, NVAR, NLEV, NLEV)
    spread_part = jnp.clip(jax.random.normal(first_key, shape_full, jnp.float32), -4.0, 4.0)
    off_diagonal = spread_part * (0.5 / math.sqrt(NLEV))
    diagonal = jax.random.uniform(second_key, (NBAND, NVAR, NLEV), jnp.float32, 0.6, 1.4)
    identity = (lax.broadcasted_iota(jnp.int32, (NLEV, NLEV), 0) == lax.broadcasted_iota(jnp.int32, (NLEV, NLEV), 1)).astype(jnp.float32)
    return off_diagonal + diagonal[..., None] * identity


def place_ends(values, key, least, high):
    place = [jax.random.randint(jax.random.fold_in(key, axis), (), 0, length) for axis, length in enumerate(values.shape)]
    main_axis = values.shape.index(max(values.shape))
    neighbour = place[:main_axis] + [(place[main_axis] + 1) % values.shape[main_axis]] + place[main_axis + 1:]
    return values.at[tuple(place)].set(least).at[tuple(neighbour)].set(high)


def level_of(stream_key, shape, pieces, smallest, high):
    level, own = 1.0, jax.random.fold_in(stream_key, 6)
    for position, shards_of in pieces:
        draws = jnp.exp(jax.random.uniform(jax.random.fold_in(own, position), (shards_of,), jnp.float32, smallest / len(pieces), high / len(pieces)))
        level = level * jnp.repeat(draws, shape[position] // shards_of).reshape([-1 if axis == position else 1 for axis in range(len(shape))])
    return level


def shared_out(key, own, number, rows, amount, top, bound, skew):
    sequence = jax.random.permutation(key, amount)
    heavy_load, ordinary = load_shares(amount, rows * top, bound, skew, True), load_shares(amount, rows * top, bound, skew, False)
    places = jnp.arange(amount)

    def named(tallies, rotation):
        used = int((tallies > 0).sum())
        fixed = max(1, used // 4)
        passed = fixed + (places - fixed + rotation * (used - fixed)) % max(1, amount - fixed)
        return jnp.zeros((amount,), jnp.int32).at[sequence[jnp.where(places < fixed, places, passed)]].set(jnp.asarray(tallies, jnp.int32))

    tallies = jnp.where(number % 4 == 0, named(heavy_load, number // 4), named(ordinary, number - number // 4 - 1))
    mixed = jax.random.permutation(jax.random.fold_in(own, 3), amount)
    source_of, sink = mixed[0:amount // 2 * 2:2], mixed[1:amount // 2 * 2:2]
    room = jnp.minimum(tallies[source_of] - 1, bound - tallies[sink]) // 2
    room = jnp.where((source_of == sequence[0]) | (sink == sequence[0]) | (tallies[sink] == 0), 0, jnp.maximum(room, 0))
    passed = jax.random.randint(jax.random.fold_in(own, 4), (amount // 2,), 0, 1 << 20) % (room + 1)
    tallies = tallies.at[source_of].add(-passed).at[sink].add(passed)
    labels = jnp.searchsorted(jnp.cumsum(tallies), jnp.arange(rows * top), side="right").astype(jnp.int32)
    table = labels.reshape(top, rows).T
    table = table[jax.random.permutation(jax.random.fold_in(own, 1), rows)]
    rotation = jax.random.randint(jax.random.fold_in(own, 2), (rows, 1), 0, top)
    return jnp.take_along_axis(table, (jnp.arange(top)[None, :] + rotation) % top, axis=1)


def load_shares(count, total, limit, slope, full):
    weights = [(1 << 20) // math.isqrt(standing ** slope) + 1 for standing in range(1, count + 1)]
    largest = limit if full else min(limit, max(-(-total // count), total * weights[0] // sum(weights)))
    least = 1 if total - largest >= count - 1 else 0
    holding, surplus = [largest] + [least] * (count - 1), total - largest - least * (count - 1)
    while surplus > 0:
        candidates = [i for i in range(1, count) if holding[i] < largest] or [i for i in range(1, count) if holding[i] < limit]
        mass, budget = sum([weights[i] for i in candidates]), surplus
        for i in candidates:
            addition = min(limit - holding[i], max(1, budget * weights[i] // mass), surplus)
            holding[i] = holding[i] + addition
            surplus = surplus - addition
    return np.array(holding)


def gaussian(stream_key, dims, scale, limit, split=(), kind=jnp.bfloat16):
    gain = level_of(stream_key, dims, split, -0.22, 0.18) if split else 1.0
    drawn = jax.random.normal(stream_key, dims, jnp.float32) * scale * gain
    return jnp.minimum(jnp.maximum(drawn, -limit), limit).astype(kind)


def setup_inputs(seed: int = 0) -> dict:
    keys = jax.random.split(jax.random.key(seed), 14)
    control_static = gaussian(keys[0], (NVAR, NLEV, NLON, LAT), 1.0, 6.0, ((1, 4), (2, 8)), jnp.float32)
    control_ens = gaussian(keys[1], (ENS, NLEV, NLON, LAT), 1.0, 6.0, ((1, 4), (2, 8)), jnp.float32)
    ens_perts = gaussian(keys[2], (ENS, NVAR, NLEV, NLON, LAT), 0.35, 2.5, ((2, 4), (3, 8)))
    band_sqrt = draw_band_sqrt(jax.random.fold_in(keys[13], 71), 0)
    band_owner = jax.random.permutation(keys[4], NBAND).astype(jnp.int32)
    scale_class = place_ends(jax.random.randint(keys[5], (NLON, LAT), 0, NCLS), jax.random.fold_in(keys[5], 1), 0, NCLS - 1).astype(jnp.int32)
    static_scales = jnp.clip(jnp.exp(jax.random.uniform(keys[6], (NCLS,), jnp.float32, math.log(0.5), math.log(4.0))), 0.5, 4.0)
    local_scales = jnp.clip(jnp.exp(jax.random.uniform(keys[7], (NCLS,), jnp.float32, math.log(1.0), math.log(8.0))), 1.0, 8.0)
    obs_source_keys = jax.random.split(jax.random.fold_in(keys[8], 1), NOBS // OBS_DEV)
    obs_source_turns = jax.random.permutation(jax.random.fold_in(keys[8], 3), NOBS // OBS_DEV)
    obs_source = jax.vmap(lambda own, number: shared_out(jax.random.fold_in(keys[8], 2), own, number, OBS_DEV, N_TILE, 1, CAP, 2))(obs_source_keys, obs_source_turns).reshape((NOBS, 1))
    obs_column = place_ends(jax.random.randint(keys[9], (NOBS,), 0, LON_DEV * LAT), jax.random.fold_in(keys[9], 1), 0, (LON_DEV * LAT) - 1).astype(jnp.int32)
    obs_jac = gaussian(keys[10], (N_TILE, NCH, NVAR, NLEV), (NVAR * NLEV) ** -0.5, 0.375, ((0, 8), (3, 4)), jnp.float32)
    innovation = gaussian(keys[11], (NCH, NOBS), 1.0, 6.0, ((1, 8),), jnp.float32)
    obs_weight = jnp.clip(jnp.exp(math.log(5.0) - 3.218876 * jax.random.uniform(keys[12], (NCH, NOBS), jnp.float32) ** level_of(keys[12], (NCH, NOBS), ((1, 8),), -0.2, 0.2)), 0.2, 5.0)
    return {"control_static": control_static, "control_ens": control_ens, "ens_perts": ens_perts, "band_sqrt": band_sqrt, "band_owner": band_owner, "scale_class": scale_class, "static_scales": static_scales, "local_scales": local_scales, "obs_source": obs_source, "obs_column": obs_column, "obs_jac": obs_jac, "innovation": innovation, "obs_weight": obs_weight}


beta_static = 0.8
beta_ensemble = 0.6
step_length = 0.3
highest = lax.Precision.HIGHEST

def face_weights(kappas):
    eastward = 0.5 * (kappas + jnp.roll(kappas, -1, axis=1))
    westward = jnp.roll(eastward, 1, axis=1)
    interior = 0.5 * (kappas[:, :, :-1] + kappas[:, :, 1:])
    edge_zero = jnp.zeros(kappas.shape[:2] + (1,), jnp.float32)
    northward = jnp.concatenate([interior, edge_zero], axis=2)
    southward = jnp.concatenate([edge_zero, interior], axis=2)
    inverse_diag = 1.0 / (1.0 + eastward + westward + northward + southward)
    return (eastward, westward, northward, southward, inverse_diag)

def per_row(weights, static_rows, member_rows):

    def spread_rows(kind_field):
        first = jnp.broadcast_to(kind_field[0:1], (static_rows,) + kind_field.shape[1:])
        second = jnp.broadcast_to(kind_field[1:2], (member_rows,) + kind_field.shape[1:])
        return jnp.concatenate([first, second], axis=0)[:, None]
    return tuple((spread_rows(kind_field) for kind_field in weights))

def lateral(state_field, weights):
    edge_zero = jnp.zeros(state_field.shape[:-1] + (1,), jnp.float32)
    upward = jnp.concatenate([state_field[..., 1:], edge_zero], axis=-1)
    downward = jnp.concatenate([edge_zero, state_field[..., :-1]], axis=-1)
    return weights[2] * upward + weights[3] * downward

def neighbours(state_field, weights):
    return weights[0] * jnp.roll(state_field, -1, axis=2) + weights[1] * jnp.roll(state_field, 1, axis=2) + lateral(state_field, weights)

def diffuse(source_field, weights):
    current = source_field
    for sweep_index in range(NSWEEP):
        current = weights[4] * (source_field + neighbours(current, weights))
    return current

def vertical(state_field, matrices):
    shaped = state_field.reshape(NVAR, NLEV, NLON, NBAND, LAT // NBAND)
    mixed_rows = jnp.einsum('bvlm,vmxbr->vlxbr', matrices, shaped, precision=highest)
    return mixed_rows.reshape(NVAR, NLEV, NLON, LAT)

def reference(control_static, control_ens, ens_perts, band_sqrt, band_owner, scale_class, static_scales, local_scales, obs_source, obs_column, obs_jac, innovation, obs_weight):
    kappas = jnp.stack([static_scales[scale_class], local_scales[scale_class]])
    weights = per_row(face_weights(kappas), NVAR, ENS)
    matrices = band_sqrt[band_owner]
    members = ens_perts.astype(jnp.float32)
    columns_global = (obs_source[:, 0] * (LON_DEV * LAT) + obs_column).astype(jnp.int32)
    jacobian = obs_jac.reshape(N_TILE, NCH, NVAR * NLEV)

    def increment(static_part, ensemble_part):
        stacked = jnp.concatenate([vertical(static_part, matrices), ensemble_part], axis=0)
        smoothed = diffuse(stacked, weights)
        return beta_static * smoothed[:NVAR] + beta_ensemble * lax.optimization_barrier(jnp.sum(members * smoothed[NVAR:, None], axis=0))

    def misfit(static_part, ensemble_part):
        state = increment(static_part, ensemble_part)
        flattened = state.reshape(NVAR * NLEV, NLON * LAT)
        picked = jnp.take(flattened, columns_global, axis=1).reshape(NVAR * NLEV, N_TILE, OBS_DEV)
        observed = jnp.einsum('tcj,jto->cto', jacobian, picked, precision=highest).reshape(NCH, N_TILE * OBS_DEV)
        departure = observed - innovation
        control_term = jnp.sum(static_part * static_part) + jnp.sum(ensemble_part * ensemble_part)
        return 0.5 * control_term + 0.5 * jnp.sum(obs_weight * departure * departure)
    gradient = jax.grad(misfit, argnums=(0, 1))
    static_part = control_static
    ensemble_part = control_ens
    for iteration in range(ITERS):
        grad_static, grad_ensemble = gradient(static_part, ensemble_part)
        static_part = static_part - step_length * grad_static
        ensemble_part = ensemble_part - step_length * grad_ensemble
    return (increment(static_part, ensemble_part), static_part, ensemble_part)
```

```python
import jax
import jax.numpy as jnp
from jax import lax
from jax.sharding import PartitionSpec as P

NSWEEP = 4
ITERS = 2

beta_static = 0.8
beta_ensemble = 0.6
step_length = 0.3
highest = lax.Precision.HIGHEST


def beside(value, axis, dim, width):
    peers, length = lax.axis_size(axis), value.shape[dim]
    up = [(i, (i + 1) % peers) for i in range(peers)]
    down = [(j, i) for i, j in up]
    before = lax.ppermute(lax.slice_in_dim(value, length - width, length, axis=dim), axis, up)
    after = lax.ppermute(lax.slice_in_dim(value, 0, width, axis=dim), axis, down)
    return before, after


def padded(value, dim, width):
    before, after = beside(value, "tile", dim, width)
    return jnp.concatenate([before, value, after], axis=dim)


def split2(value):
    high = lax.reduce_precision(value, 8, 7)
    return high.astype(jnp.bfloat16), (value - high).astype(jnp.bfloat16)


def lateral(field, weights):
    edge_zero = jnp.zeros(field.shape[:-1] + (1,), jnp.float32)
    upward = jnp.concatenate([field[..., 1:], edge_zero], axis=-1)
    downward = jnp.concatenate([edge_zero, field[..., :-1]], axis=-1)
    return weights[2] * upward + weights[3] * downward


def neighbours(wide, weights):
    return (
        weights[0] * wide[:, 2:]
        + weights[1] * wide[:, :-2]
        + lateral(wide[:, 1:-1], weights)
    )


def cut(weights, start, count):
    return [w[start:start + count] for w in weights]


def diffuse(wide, weights, lons):
    current = wide
    for sweep in range(1, NSWEEP + 1):
        count = lons + 2 * (NSWEEP - sweep)
        here = cut(weights, sweep, count)
        current = here[4] * (wide[:, sweep:sweep + count] + neighbours(current, here))
    return current


def diffuse_back(wide, weights, lons):
    total = 0.0
    carried = wide
    for sweep in range(NSWEEP):
        count = lons + 2 * (NSWEEP - sweep)
        scaled = cut(weights, sweep, count)[4] * carried
        inner = NSWEEP - sweep
        total = total + scaled[:, inner:inner + lons]
        carried = neighbours(scaled, cut(weights, sweep + 1, count - 2))
    return total + carried


def on_device(
    control_static,
    control_ens,
    ens_perts,
    band_sqrt,
    band_owner,
    scale_class,
    static_scales,
    local_scales,
    obs_source,
    obs_column,
    obs_jac,
    innovation,
    obs_weight,
):
    tiles = lax.axis_size("tile")
    levs = lax.axis_size("lev")
    lev_index = lax.axis_index("lev")
    variables, levels, lons, lats = control_static.shape
    members = control_ens.shape[0]
    all_levels = band_sqrt.shape[3]
    bands = band_owner.shape[0]
    height = lats // bands
    classes = static_scales.shape[0]
    columns = lons * lats
    channels = obs_jac.shape[1]
    obs_total = obs_column.shape[0]
    capacity = max(2, 4 * obs_total // tiles)
    share = channels // levs

    tables = jnp.stack([static_scales, local_scales])
    marks = (
        scale_class[None] == lax.broadcasted_iota(jnp.int32, (classes, lons, lats), 0)
    ).astype(jnp.float32)
    kappas = jnp.sum(tables[:, :, None, None] * marks[None], axis=1)
    wide_kappas = padded(kappas, 1, NSWEEP + 1)
    centre = wide_kappas[:, 1:-1]
    eastward = 0.5 * (centre + wide_kappas[:, 2:])
    westward = 0.5 * (wide_kappas[:, :-2] + centre)
    interior = 0.5 * (centre[:, :, :-1] + centre[:, :, 1:])
    edge_zero = jnp.zeros((2, centre.shape[1], 1), jnp.float32)
    northward = jnp.concatenate([interior, edge_zero], axis=2)
    southward = jnp.concatenate([edge_zero, interior], axis=2)
    inverse_diag = 1.0 / (1.0 + eastward + westward + northward + southward)
    weights = (eastward, westward, northward, southward, inverse_diag)
    static_weights = [w[0] for w in weights]
    local_weights = [w[1] for w in weights]

    source = obs_source[:, 0]
    source_marks = source[:, None] == lax.broadcasted_iota(jnp.int32, (obs_total, tiles), 1)
    earlier = (
        lax.broadcasted_iota(jnp.int32, (obs_total, obs_total), 1)
        < lax.broadcasted_iota(jnp.int32, (obs_total, obs_total), 0)
    ).astype(jnp.bfloat16)
    before = jnp.dot(earlier, source_marks.astype(jnp.bfloat16), preferred_element_type=jnp.float32)
    slot = jnp.sum(jnp.where(source_marks, before, 0.0), axis=1).astype(jnp.int32)
    place = source * capacity + slot
    place_marks = (
        place[:, None] == lax.broadcasted_iota(jnp.int32, (obs_total, tiles * capacity), 1)
    ).astype(jnp.float32)
    own_share = lambda value: lax.dynamic_slice_in_dim(value, lev_index * share, share, axis=0)
    payload = jnp.concatenate(
        [
            own_share(obs_weight),
            own_share(innovation),
            jnp.broadcast_to(obs_column.astype(jnp.float32)[None], (8, obs_total)),
        ],
        axis=0,
    )
    outgoing = jnp.dot(payload, place_marks, precision=highest)
    arrived = lax.all_to_all(outgoing, "tile", split_axis=1, concat_axis=1, tiled=True)
    slots = tiles * capacity
    seen = arrived[2 * share].astype(jnp.int32)
    column_marks = (
        lax.broadcasted_iota(jnp.int32, (columns, slots), 0) == seen[None]
    ).astype(jnp.bfloat16)
    pair = lax.all_gather(arrived[:2 * share], "lev", axis=0, tiled=True)
    pair = pair.reshape(levs, 2, share, tiles, capacity).transpose(1, 3, 0, 2, 4)
    pair = pair.reshape(2, tiles, channels, capacity)
    slot_weight, slot_innovation = pair[0], pair[1]

    own_jac = obs_jac[0].reshape(channels, variables * levels)
    jacs = lax.all_gather(own_jac, "tile", axis=0)
    all_jacs = lax.all_gather(jacs, "lev", axis=2, tiled=True)

    own_rows = lax.all_gather(band_sqrt, "tile", axis=0, tiled=True)
    own_rows = jnp.take(own_rows, band_owner, axis=0)
    roots = lax.all_gather(own_rows, "lev", axis=2, tiled=True)
    own_columns = lax.dynamic_slice_in_dim(roots, lev_index * levels, levels, axis=3)
    squares = jnp.einsum("bvlm,bvkm->bvlk", own_rows, roots, precision=highest)
    update = jnp.concatenate([own_columns.transpose(0, 1, 3, 2), squares], axis=2)

    def vertical(matrices, full):
        shaped = full.reshape(variables, all_levels, lons, bands, height)
        result = jnp.einsum("bvlm,vmxbr->vlxbr", matrices, shaped, precision=highest)
        return result.reshape(variables, matrices.shape[2], lons, lats)

    perts = ens_perts.astype(jnp.float32)

    def increment(mixed, ensemble):
        stacked = jnp.concatenate([mixed, ensemble], axis=0).reshape(-1, lons, lats)
        wide = padded(stacked, 1, NSWEEP)
        rows = variables * levels
        first = diffuse(wide[:rows], static_weights, lons).reshape(control_static.shape)
        second = diffuse(wide[rows:], local_weights, lons).reshape(control_ens.shape)
        return beta_static * first + beta_ensemble * jnp.sum(perts * second[:, None], axis=0)

    static, ensemble = control_static, control_ens
    mixed = vertical(own_rows, lax.all_gather(static, "lev", axis=1, tiled=True))
    for iteration in range(ITERS):
        state = increment(mixed, ensemble).reshape(variables * levels, columns)
        full = lax.all_gather(state, "lev", axis=0, tiled=True)
        high, low = split2(full)
        picked = jnp.dot(jnp.concatenate([high, low], axis=0), column_marks,
                         preferred_element_type=jnp.float32)
        picked = (picked[:full.shape[0]] + picked[full.shape[0]:]).reshape(-1, tiles, capacity)
        observed = jnp.einsum("tcj,jto->tco", all_jacs, picked, precision=highest)
        weighted = slot_weight * (observed - slot_innovation)
        pulled = jnp.einsum("tcj,tco->jto", jacs, weighted, precision=highest)
        pulled = pulled.reshape(-1, slots)
        high, low = split2(pulled)
        gradient = lax.dot_general(
            jnp.concatenate([high, low], axis=0), column_marks, (((1,), (1,)), ((), ())),
            preferred_element_type=jnp.float32,
        )
        gradient = gradient[:pulled.shape[0]] + gradient[pulled.shape[0]:]
        gradient = gradient.reshape(control_static.shape)
        member_gradient = beta_ensemble * jnp.sum(perts * gradient[None], axis=1)
        stacked = jnp.concatenate([beta_static * gradient, member_gradient], axis=0)
        wide = padded(stacked.reshape(-1, lons, lats), 1, NSWEEP)
        rows = variables * levels
        static_back = diffuse_back(wide[:rows], static_weights, lons).reshape(control_static.shape)
        local_back = diffuse_back(wide[rows:], local_weights, lons).reshape(control_ens.shape)
        steps = vertical(update, lax.all_gather(static_back, "lev", axis=1, tiled=True))
        static = static - step_length * (static + steps[:, :levels])
        mixed = mixed - step_length * (mixed + steps[:, levels:])
        ensemble = ensemble - step_length * (ensemble + local_back)
    return (increment(mixed, ensemble), static, ensemble)


def solution(mesh):
    return jax.shard_map(
        on_device,
        mesh=mesh,
        in_specs=(
            P(None, "lev", "tile", None),
            P(None, "lev", "tile", None),
            P(None, None, "lev", "tile", None),
            P("tile", None, "lev", None),
            P(),
            P("tile", None),
            P(),
            P(),
            P("tile", None),
            P("tile"),
            P("tile", None, None, "lev"),
            P(None, "tile"),
            P(None, "tile"),
        ),
        out_specs=(
            P(None, "lev", "tile", None),
            P(None, "lev", "tile", None),
            P(None, "lev", "tile", None),
        ),
        check_vma=False,
    )
```

```python
import functools

import jax
import jax.numpy as jnp
from jax import lax
from jax.experimental import pallas as pl
from jax.experimental.pallas import tpu as pltpu
from jax.sharding import PartitionSpec as P

NSWEEP = 4
ITERS = 2

beta_static = 0.8
beta_ensemble = 0.6
step_length = 0.3
highest = lax.Precision.HIGHEST
MESH = pl.DeviceIdType.MESH
GROUP = 4
vmem = pl.BlockSpec(memory_space=pltpu.VMEM)


def beside(value, axis, dim, width):
    peers, length = lax.axis_size(axis), value.shape[dim]
    up = [(i, (i + 1) % peers) for i in range(peers)]
    down = [(j, i) for i, j in up]
    before = lax.ppermute(lax.slice_in_dim(value, length - width, length, axis=dim), axis, up)
    after = lax.ppermute(lax.slice_in_dim(value, 0, width, axis=dim), axis, down)
    return before, after


def padded(value, dim, width):
    before, after = beside(value, "tile", dim, width)
    return jnp.concatenate([before, value, after], axis=dim)


def split2(value):
    high = lax.reduce_precision(value, 8, 7)
    return high.astype(jnp.bfloat16), (value - high).astype(jnp.bfloat16)


def greet(peers):
    barrier = pltpu.get_barrier_semaphore()
    for peer in peers:
        pl.semaphore_signal(barrier, inc=1, device_id=peer, device_id_type=MESH)
    pl.semaphore_wait(barrier, len(peers))


def tile_peers():
    tiles, me = lax.axis_size("tile"), lax.axis_index("tile")
    return {"tile": lax.rem(me + tiles - 1, tiles)}, {"tile": lax.rem(me + 1, tiles)}


def lev_peers():
    me = lax.axis_index("lev")
    core = lax.rem(me, 2)
    return me, me + 1 - 2 * core, me + 2 - 4 * (me // 2)


def halo_copies(field, halo, index, send, recv):
    left, right = tile_peers()
    half = NSWEEP
    copies = []
    for side, peer in ((0, left), (1, right)):
        part = pl.ds(side * half, half)
        copies.append(
            pltpu.make_async_remote_copy(
                src_ref=field.at[:, part, :],
                dst_ref=halo.at[index, :, part, :],
                send_sem=send.at[index, side],
                recv_sem=recv.at[index, side],
                device_id=peer,
                device_id_type=MESH,
            )
        )
    return copies


def spread_copies(full, var, send, recv):
    me, core_peer, chip_peer = lev_peers()
    plan = ((me, core_peer), (me, chip_peer), (chip_peer, core_peer))
    return [
        pltpu.make_async_remote_copy(
            src_ref=full.at[block, var],
            dst_ref=full.at[block, var],
            send_sem=send.at[var, kind],
            recv_sem=recv.at[var, kind],
            device_id={"lev": peer},
            device_id_type=MESH,
        )
        for kind, (block, peer) in enumerate(plan)
    ]


def shifted(value):
    lons, lats = value.shape[1:]
    return (
        pltpu.roll(value, lons - 1, 1),
        pltpu.roll(value, 1, 1),
        pltpu.roll(value, lats - 1, 2),
        pltpu.roll(value, 1, 2),
    )


def neighbours(value, weights):
    east, west, north, south = shifted(value)
    return weights[0] * east + weights[1] * west + (weights[2] * north + weights[3] * south)


def kind_weights(w_ref, kind):
    return [w_ref[kind, i][None] for i in range(5)]


def over_rows(levels, body):
    def step(i, carry):
        body(pl.ds(pl.multiple_of(i * GROUP, GROUP), GROUP))
        return carry

    lax.fori_loop(0, levels // GROUP, step, 0)


def forward_rows(source, weights):
    current = source
    for sweep in range(NSWEEP):
        current = weights[4] * (source + neighbours(current, weights))
    return current


def backward_rows(source, weights):
    total, carried = jnp.zeros_like(source), source
    for sweep in range(NSWEEP):
        scaled = weights[4] * carried
        total = total + scaled
        carried = neighbours(scaled, weights)
    return total + carried


def forward_kernel(spread, mixed, ensemble, perts, w_ref, out, halo, hsend, hrecv, lsend, lrecv):
    variables, levels, lons, _ = mixed.shape
    members = ensemble.shape[0]
    me, core_peer, chip_peer = lev_peers()
    greet(tile_peers() + (({"lev": core_peer}, {"lev": chip_peer}) if spread else ()))
    copies = [halo_copies(mixed.at[v], halo, v, hsend, hrecv) for v in range(variables)]
    copies += [
        halo_copies(ensemble.at[e], halo, variables + e, hsend, hrecv) for e in range(members)
    ]
    for pair in copies:
        for copy in pair:
            copy.start()
    block = out.at[me] if spread else out
    for field in range(variables + members):
        for copy in copies[field]:
            copy.wait_recv()
        static = field < variables
        weights = kind_weights(w_ref, 0 if static else 1)
        own = mixed.at[field] if static else ensemble.at[field - variables]

        def body(rows):
            value = jnp.concatenate([own[rows], halo[field, rows]], axis=1)
            result = forward_rows(value, weights)[:, :lons]
            if static:
                block[field, rows] = beta_static * result
            else:
                result = beta_ensemble * result
                for v in range(variables):
                    block[v, rows] += perts[field - variables, v, rows] * result

        over_rows(levels, body)
    if spread:
        plans = [spread_copies(out, v, lsend, lrecv) for v in range(variables)]
        finish_spread(plans, start=True)
    for pair in copies:
        for copy in pair:
            copy.wait_send()


def finish_spread(plans, start):
    if start:
        for plan in plans:
            plan[1].start()
            plan[0].start()
    for plan in plans:
        plan[1].wait_recv()
        plan[2].start()
    for plan in plans:
        plan[0].wait_recv()
        plan[2].wait_recv()
        for copy in plan:
            copy.wait_send()


def backward_kernel(
    gradient, ensemble, perts, w_ref, full, updated, source, halo, hsend, hrecv, lsend, lrecv
):
    variables, levels, lons, _ = gradient.shape
    members = ensemble.shape[0]
    me, core_peer, chip_peer = lev_peers()
    greet(tile_peers() + ({"lev": core_peer}, {"lev": chip_peer}))

    def mix(rows):
        parts = [gradient[v, rows] for v in range(variables)]
        for v in range(variables):
            source[v, rows] = beta_static * parts[v]
        for e in range(members):
            total = perts[e, 0, rows] * parts[0]
            for v in range(1, variables):
                total = total + perts[e, v, rows] * parts[v]
            source[variables + e, rows] = beta_ensemble * total

    over_rows(levels, mix)
    copies = [
        halo_copies(source.at[f], halo, f, hsend, hrecv) for f in range(variables + members)
    ]
    for pair in copies:
        for copy in pair:
            copy.start()
    plans = [spread_copies(full, v, lsend, lrecv) for v in range(variables)]
    for field in range(variables + members):
        for copy in copies[field]:
            copy.wait_recv()
        static = field < variables
        weights = kind_weights(w_ref, 0 if static else 1)

        def body(rows):
            value = jnp.concatenate([source[field, rows], halo[field, rows]], axis=1)
            result = backward_rows(value, weights)[:, :lons]
            if static:
                full[me, field, rows] = result
            else:
                held = ensemble[field - variables, rows]
                updated[field - variables, rows] = held - step_length * (held + result)

        over_rows(levels, body)
        if static:
            plans[field][1].start()
            plans[field][0].start()
    finish_spread(plans, start=False)
    for pair in copies:
        for copy in pair:
            copy.wait_send()


def exchange_kernel(matrix, jacobian, payload, matrices, jacobians, arrived, send, recv):
    tiles, me = lax.axis_size("tile"), lax.axis_index("tile")
    barrier = pltpu.get_barrier_semaphore()

    def signal(offset, carry):
        peer = lax.rem(me + offset, tiles)
        pl.semaphore_signal(barrier, inc=1, device_id={"tile": peer}, device_id_type=MESH)
        return carry

    lax.fori_loop(1, tiles, signal, 0)
    pl.semaphore_wait(barrier, tiles - 1)

    def copies(offset):
        peer = lax.rem(me + offset, tiles)
        pairs = (
            (matrix, matrices.at[me]),
            (jacobian, jacobians.at[me]),
            (payload.at[peer], arrived.at[me]),
        )
        return [
            pltpu.make_async_remote_copy(
                src_ref=src,
                dst_ref=dst,
                send_sem=send.at[k, offset],
                recv_sem=recv.at[k, offset],
                device_id={"tile": peer},
                device_id_type=MESH,
            )
            for k, (src, dst) in enumerate(pairs)
        ]

    def begin(offset, carry):
        for copy in copies(offset):
            copy.start()
        return carry

    lax.fori_loop(1, tiles, begin, 0)
    matrices[me] = matrix[...]
    jacobians[me] = jacobian[...]
    arrived[me] = payload[me]

    def finish(offset, carry):
        for copy in copies(offset):
            copy.wait()
        return carry

    lax.fori_loop(1, tiles, finish, 0)


def call(kernel, name, identity, shapes, scratch, *operands):
    many = isinstance(shapes, list)
    result = pl.pallas_call(
        kernel,
        name=name,
        out_shape=shapes if many else [shapes],
        in_specs=[vmem] * len(operands),
        out_specs=[vmem] * (len(shapes) if many else 1),
        scratch_shapes=scratch,
        compiler_params=pltpu.CompilerParams(
            collective_id=identity, has_side_effects=True, vmem_limit_bytes=40 * 2**20
        ),
    )(*operands)
    return result if many else result[0]


def on_device(
    control_static,
    control_ens,
    ens_perts,
    band_sqrt,
    band_owner,
    scale_class,
    static_scales,
    local_scales,
    obs_source,
    obs_column,
    obs_jac,
    innovation,
    obs_weight,
):
    tiles = lax.axis_size("tile")
    levs = lax.axis_size("lev")
    lev_index = lax.axis_index("lev")
    variables, levels, lons, lats = control_static.shape
    members = control_ens.shape[0]
    all_levels = band_sqrt.shape[3]
    bands = band_owner.shape[0]
    height = lats // bands
    classes = static_scales.shape[0]
    columns = lons * lats
    channels = obs_jac.shape[1]
    obs_total = obs_column.shape[0]
    capacity = max(2, 4 * obs_total // tiles)
    share = channels // levs

    tables = jnp.stack([static_scales, local_scales])
    marks = (
        scale_class[None] == lax.broadcasted_iota(jnp.int32, (classes, lons, lats), 0)
    ).astype(jnp.float32)
    kappas = jnp.sum(tables[:, :, None, None] * marks[None], axis=1)
    wide_kappas = padded(kappas, 1, NSWEEP + 1)
    centre = wide_kappas[:, 1:-1]
    eastward = 0.5 * (centre + wide_kappas[:, 2:])
    westward = 0.5 * (wide_kappas[:, :-2] + centre)
    interior = 0.5 * (centre[:, :, :-1] + centre[:, :, 1:])
    edge_zero = jnp.zeros((2, centre.shape[1], 1), jnp.float32)
    northward = jnp.concatenate([interior, edge_zero], axis=2)
    southward = jnp.concatenate([edge_zero, interior], axis=2)
    inverse_diag = 1.0 / (1.0 + eastward + westward + northward + southward)
    weights = (eastward, westward, northward, southward, inverse_diag)
    wide_weights = jnp.roll(jnp.stack(weights, axis=1), -NSWEEP, axis=2)

    source = obs_source[:, 0]
    source_marks = source[:, None] == lax.broadcasted_iota(jnp.int32, (obs_total, tiles), 1)
    earlier = (
        lax.broadcasted_iota(jnp.int32, (obs_total, obs_total), 1)
        < lax.broadcasted_iota(jnp.int32, (obs_total, obs_total), 0)
    ).astype(jnp.bfloat16)
    before = jnp.dot(earlier, source_marks.astype(jnp.bfloat16), preferred_element_type=jnp.float32)
    slot = jnp.sum(jnp.where(source_marks, before, 0.0), axis=1).astype(jnp.int32)
    place = source * capacity + slot
    place_marks = (
        place[:, None] == lax.broadcasted_iota(jnp.int32, (obs_total, tiles * capacity), 1)
    ).astype(jnp.float32)
    own_share = lambda value: lax.dynamic_slice_in_dim(value, lev_index * share, share, axis=0)
    payload = jnp.concatenate(
        [
            own_share(obs_weight),
            own_share(innovation),
            jnp.broadcast_to(obs_column.astype(jnp.float32)[None], (8, obs_total)),
        ],
        axis=0,
    )
    outgoing = jnp.dot(payload, place_marks, precision=highest)
    outgoing = outgoing.reshape(payload.shape[0], tiles, capacity).transpose(1, 0, 2)
    own_jac = obs_jac[0].reshape(channels, variables * levels)
    shape = lambda *dims: jax.ShapeDtypeStruct(dims, jnp.float32)
    own_rows, jacs, arrived = call(
        exchange_kernel, "exchange", 0,
        [shape(tiles, *band_sqrt.shape[1:]), shape(tiles, *own_jac.shape), shape(*outgoing.shape)],
        [pltpu.SemaphoreType.DMA((3, tiles)), pltpu.SemaphoreType.DMA((3, tiles))],
        band_sqrt[0], own_jac, outgoing,
    )
    arrived = arrived.transpose(1, 0, 2).reshape(payload.shape[0], tiles * capacity)
    slots = tiles * capacity
    seen = arrived[2 * share].astype(jnp.int32)
    column_marks = (
        lax.broadcasted_iota(jnp.int32, (columns, slots), 0) == seen[None]
    ).astype(jnp.bfloat16)
    pair = lax.all_gather(arrived[:2 * share], "lev", axis=0, tiled=True)
    pair = pair.reshape(levs, 2, share, tiles, capacity).transpose(1, 3, 0, 2, 4)
    pair = pair.reshape(2, tiles, channels, capacity)
    slot_weight, slot_innovation = pair[0], pair[1]

    all_jacs = lax.all_gather(jacs, "lev", axis=2, tiled=True)

    own_rows = jnp.take(own_rows, band_owner, axis=0)
    roots = lax.all_gather(own_rows, "lev", axis=2, tiled=True)
    own_columns = lax.dynamic_slice_in_dim(roots, lev_index * levels, levels, axis=3)
    squares = jnp.einsum("bvlm,bvkm->bvlk", own_rows, roots, precision=highest)
    update = jnp.concatenate([own_columns.transpose(0, 1, 3, 2), squares], axis=2)

    def vertical(matrices, full):
        shaped = full.reshape(variables, all_levels, lons, bands, height)
        result = jnp.einsum("bvlm,vmxbr->vlxbr", matrices, shaped, precision=highest)
        return result.reshape(variables, matrices.shape[2], lons, lats)

    perts = ens_perts.astype(jnp.float32)

    fields = variables + members
    halo = pltpu.VMEM((fields, levels, lons, lats), jnp.float32)
    halo_sems = [pltpu.SemaphoreType.DMA((fields, 2))] * 2
    lev_sems = [pltpu.SemaphoreType.DMA((variables, 3))] * 2
    block = (variables, levels, lons, lats)

    def increment(mixed, ensemble, spread):
        return call(
            functools.partial(forward_kernel, spread), "forward", 1 if spread else 2,
            shape(levs, *block) if spread else shape(*block),
            [halo] + halo_sems + lev_sems, mixed, ensemble, perts, wide_weights,
        )

    static, ensemble = control_static, control_ens
    mixed = vertical(own_rows, lax.all_gather(static, "lev", axis=1, tiled=True))
    for iteration in range(ITERS):
        full = increment(mixed, ensemble, True).reshape(levs * variables * levels, columns)
        high, low = split2(full)
        picked = jnp.dot(jnp.concatenate([high, low], axis=0), column_marks,
                         preferred_element_type=jnp.float32)
        picked = (picked[:full.shape[0]] + picked[full.shape[0]:]).reshape(-1, tiles, capacity)
        observed = jnp.einsum("tcj,jto->tco", all_jacs, picked, precision=highest)
        weighted = slot_weight * (observed - slot_innovation)
        pulled = jnp.einsum("tcj,tco->jto", jacs, weighted, precision=highest)
        pulled = pulled.reshape(-1, slots)
        high, low = split2(pulled)
        gradient = lax.dot_general(
            jnp.concatenate([high, low], axis=0), column_marks, (((1,), (1,)), ((), ())),
            preferred_element_type=jnp.float32,
        )
        gradient = gradient[:pulled.shape[0]] + gradient[pulled.shape[0]:]
        gradient = gradient.reshape(control_static.shape)
        full, ensemble = call(
            backward_kernel, "backward", 3, [shape(levs, *block), shape(*control_ens.shape)],
            [halo, halo] + halo_sems + lev_sems, gradient, ensemble, perts, wide_weights,
        )
        full = full.transpose(1, 0, 2, 3, 4).reshape(variables, all_levels, lons, lats)
        steps = vertical(update, full)
        static = static - step_length * (static + steps[:, :levels])
        mixed = mixed - step_length * (mixed + steps[:, levels:])
    return (increment(mixed, ensemble, False), static, ensemble)


def solution(mesh):
    return jax.shard_map(
        on_device,
        mesh=mesh,
        in_specs=(
            P(None, "lev", "tile", None),
            P(None, "lev", "tile", None),
            P(None, None, "lev", "tile", None),
            P("tile", None, "lev", None),
            P(),
            P("tile", None),
            P(),
            P(),
            P("tile", None),
            P("tile"),
            P("tile", None, None, "lev"),
            P(None, "tile"),
            P(None, "tile"),
        ),
        out_specs=(
            P(None, "lev", "tile", None),
            P(None, "lev", "tile", None),
            P(None, "lev", "tile", None),
        ),
        check_vma=False,
    )
```

```python
import functools

import jax
import jax.numpy as jnp
from jax import lax
from jax.experimental import pallas as pl
from jax.experimental.pallas import tpu as pltpu
from jax.sharding import PartitionSpec as P

NSWEEP = 4
ITERS = 2

beta_static = 0.8
beta_ensemble = 0.6
step_length = 0.3
highest = lax.Precision.HIGHEST
MESH = pl.DeviceIdType.MESH
GROUP = 8
vmem = pl.BlockSpec(memory_space=pltpu.VMEM)


def split2(value):
    high = lax.reduce_precision(value, 8, 7)
    return high.astype(jnp.bfloat16), (value - high).astype(jnp.bfloat16)


def greet(peers):
    barrier = pltpu.get_barrier_semaphore()
    for peer in peers:
        pl.semaphore_signal(barrier, inc=1, device_id=peer, device_id_type=MESH)
    pl.semaphore_wait(barrier, len(peers))


def tile_peers():
    tiles, me = lax.axis_size("tile"), lax.axis_index("tile")
    return {"tile": lax.rem(me + tiles - 1, tiles)}, {"tile": lax.rem(me + 1, tiles)}


def lev_peers():
    me = lax.axis_index("lev")
    core = lax.rem(me, 2)
    return me, me + 1 - 2 * core, me + 2 - 4 * (me // 2)


def halo_copies(field, halo, index, send, recv):
    left, right = tile_peers()
    half, lons = NSWEEP, field.shape[0]
    copies = []
    for side, peer, start in ((1, left, 0), (0, right, lons - half)):
        copies.append(
            pltpu.make_async_remote_copy(
                src_ref=field.at[pl.ds(start, half)],
                dst_ref=halo.at[index, pl.ds(side * half, half)],
                send_sem=send.at[index, side],
                recv_sem=recv.at[index, side],
                device_id=peer,
                device_id_type=MESH,
            )
        )
    return copies


def spread_copies(full, var, send, recv):
    me, core_peer, chip_peer = lev_peers()
    plan = ((me, core_peer), (me, chip_peer), (chip_peer, core_peer))
    return [
        pltpu.make_async_remote_copy(
            src_ref=full.at[block, var],
            dst_ref=full.at[block, var],
            send_sem=send.at[var, kind],
            recv_sem=recv.at[var, kind],
            device_id={"lev": peer},
            device_id_type=MESH,
        )
        for kind, (block, peer) in enumerate(plan)
    ]


def neighbours(wide, weights):
    lats = wide.shape[2]
    inner = wide[1:-1]
    return (weights[0] * wide[2:] + weights[1] * wide[:-2]) + (
        weights[2] * pltpu.roll(inner, lats - 1, 2) + weights[3] * pltpu.roll(inner, 1, 2)
    )


def kind_weights(w_ref, kind):
    return lambda i, start, count: w_ref[kind, i, pl.ds(start, count)]


def over_rows(levels, body):
    def step(i, carry):
        body(pl.ds(pl.multiple_of(i * GROUP, GROUP), GROUP))
        return carry

    lax.fori_loop(0, levels // GROUP, step, 0)


def widened(field, halo, index, rows):
    half = NSWEEP
    return jnp.concatenate(
        [halo[index, :half, rows], field[:, rows], halo[index, half:, rows]], axis=0
    )


def forward_rows(source, weights):
    current = source
    for sweep in range(1, NSWEEP + 1):
        count = source.shape[0] - 2 * sweep
        here = [weights(i, sweep, count) for i in range(5)]
        current = here[4] * (source[sweep:sweep + count] + neighbours(current, here))
    return current


def backward_rows(source, weights):
    lons = source.shape[0] - 2 * NSWEEP
    total, carried = 0.0, source
    for sweep in range(NSWEEP):
        count = source.shape[0] - 2 * sweep
        scaled = weights(4, sweep, count) * carried
        inner = NSWEEP - sweep
        total = total + scaled[inner:inner + lons]
        carried = neighbours(scaled, [weights(i, sweep + 1, count - 2) for i in range(4)])
    return total + carried


def forward_kernel(spread, mixed, ensemble, perts, w_ref, out, halo, hsend, hrecv, lsend, lrecv):
    variables, _, levels, _ = mixed.shape
    members = ensemble.shape[0]
    me, core_peer, chip_peer = lev_peers()
    greet(tile_peers() + (({"lev": core_peer}, {"lev": chip_peer}) if spread else ()))
    copies = [halo_copies(mixed.at[v], halo, v, hsend, hrecv) for v in range(variables)]
    copies += [
        halo_copies(ensemble.at[e], halo, variables + e, hsend, hrecv) for e in range(members)
    ]
    for pair in copies:
        for copy in pair:
            copy.start()
    block = out.at[me] if spread else out
    for field in range(variables + members):
        for copy in copies[field]:
            copy.wait_recv()
        static = field < variables
        weights = kind_weights(w_ref, 0 if static else 1)
        own = mixed.at[field] if static else ensemble.at[field - variables]

        def body(rows):
            result = forward_rows(widened(own, halo, field, rows), weights)
            if static:
                block[field, :, rows] = beta_static * result
            else:
                result = beta_ensemble * result
                for v in range(variables):
                    block[v, :, rows] += perts[field - variables, v, :, rows] * result

        over_rows(levels, body)
    if spread:
        plans = [spread_copies(out, v, lsend, lrecv) for v in range(variables)]
        finish_spread(plans, start=True)
    for pair in copies:
        for copy in pair:
            copy.wait_send()


def finish_spread(plans, start):
    if start:
        for plan in plans:
            plan[1].start()
            plan[0].start()
    for plan in plans:
        plan[1].wait_recv()
        plan[2].start()
    for plan in plans:
        plan[0].wait_recv()
        plan[2].wait_recv()
        for copy in plan:
            copy.wait_send()


def backward_kernel(
    gradient, ensemble, perts, w_ref, full, updated, source, halo, hsend, hrecv, lsend, lrecv
):
    variables, _, levels, _ = gradient.shape
    members = ensemble.shape[0]
    me, core_peer, chip_peer = lev_peers()
    greet(tile_peers() + ({"lev": core_peer}, {"lev": chip_peer}))

    def mix(rows):
        parts = [gradient[v, :, rows] for v in range(variables)]
        for v in range(variables):
            source[v, :, rows] = beta_static * parts[v]
        for e in range(members):
            total = perts[e, 0, :, rows] * parts[0]
            for v in range(1, variables):
                total = total + perts[e, v, :, rows] * parts[v]
            source[variables + e, :, rows] = beta_ensemble * total

    over_rows(levels, mix)
    copies = [
        halo_copies(source.at[f], halo, f, hsend, hrecv) for f in range(variables + members)
    ]
    for pair in copies:
        for copy in pair:
            copy.start()
    plans = [spread_copies(full, v, lsend, lrecv) for v in range(variables)]
    for field in range(variables + members):
        for copy in copies[field]:
            copy.wait_recv()
        static = field < variables
        weights = kind_weights(w_ref, 0 if static else 1)

        def body(rows):
            result = backward_rows(widened(source.at[field], halo, field, rows), weights)
            if static:
                full[me, field, :, rows] = result
            else:
                held = ensemble[field - variables, :, rows]
                updated[field - variables, :, rows] = held - step_length * (held + result)

        over_rows(levels, body)
        if static:
            plans[field][1].start()
            plans[field][0].start()
    finish_spread(plans, start=False)
    for pair in copies:
        for copy in pair:
            copy.wait_send()


def exchange_kernel(
    matrix, jacobian, kappa, payload, matrices, jacobians, kappas, arrived, send, recv
):
    tiles, me = lax.axis_size("tile"), lax.axis_index("tile")
    barrier = pltpu.get_barrier_semaphore()

    def signal(offset, carry):
        peer = lax.rem(me + offset, tiles)
        pl.semaphore_signal(barrier, inc=1, device_id={"tile": peer}, device_id_type=MESH)
        return carry

    lax.fori_loop(1, tiles, signal, 0)
    pl.semaphore_wait(barrier, tiles - 1)

    def copies(offset):
        peer = lax.rem(me + offset, tiles)
        pairs = (
            (matrix, matrices.at[me]),
            (jacobian, jacobians.at[me]),
            (kappa, kappas.at[me]),
            (payload.at[peer], arrived.at[me]),
        )
        return [
            pltpu.make_async_remote_copy(
                src_ref=src,
                dst_ref=dst,
                send_sem=send.at[k, offset],
                recv_sem=recv.at[k, offset],
                device_id={"tile": peer},
                device_id_type=MESH,
            )
            for k, (src, dst) in enumerate(pairs)
        ]

    def begin(offset, carry):
        for copy in copies(offset):
            copy.start()
        return carry

    lax.fori_loop(1, tiles, begin, 0)
    matrices[me] = matrix[...]
    jacobians[me] = jacobian[...]
    kappas[me] = kappa[...]
    arrived[me] = payload[me]

    def finish(offset, carry):
        for copy in copies(offset):
            copy.wait()
        return carry

    lax.fori_loop(1, tiles, finish, 0)


def vertical_kernel(full, matrices, static, mixed, new_static, new_mixed):
    levs, variables, lons, levels, lats = full.shape
    rows = 2 * levels
    bands = matrices.shape[1] // rows
    band = lax.broadcasted_iota(jnp.int32, (rows, lats), 1) // (lats // bands)

    def step(x, carry):
        for v in range(variables):
            column = jnp.concatenate([full[block, v, x] for block in range(levs)], axis=0)
            product = jnp.dot(
                matrices[v], column, precision=highest, preferred_element_type=jnp.float32
            )
            kept = product[:rows]
            for b in range(1, bands):
                kept = jnp.where(band == b, product[b * rows:(b + 1) * rows], kept)
            held, other = static[v, x], mixed[v, x]
            new_static[v, x] = held - step_length * (held + kept[:levels])
            new_mixed[v, x] = other - step_length * (other + kept[levels:])
        return carry

    lax.fori_loop(0, lons, step, 0)


def call(kernel, name, identity, shapes, scratch, *operands):
    many = isinstance(shapes, list)
    result = pl.pallas_call(
        kernel,
        name=name,
        out_shape=shapes if many else [shapes],
        in_specs=[vmem] * len(operands),
        out_specs=[vmem] * (len(shapes) if many else 1),
        scratch_shapes=scratch,
        compiler_params=pltpu.CompilerParams(
            collective_id=identity,
            has_side_effects=identity is not None,
            vmem_limit_bytes=40 * 2**20,
        ),
    )(*operands)
    return result if many else result[0]


def on_device(
    control_static,
    control_ens,
    ens_perts,
    band_sqrt,
    band_owner,
    scale_class,
    static_scales,
    local_scales,
    obs_source,
    obs_column,
    obs_jac,
    innovation,
    obs_weight,
):
    tiles = lax.axis_size("tile")
    levs = lax.axis_size("lev")
    lev_index = lax.axis_index("lev")
    variables, levels, lons, lats = control_static.shape
    members = control_ens.shape[0]
    all_levels = band_sqrt.shape[3]
    bands = band_owner.shape[0]
    height = lats // bands
    classes = static_scales.shape[0]
    columns = lons * lats
    channels = obs_jac.shape[1]
    obs_total = obs_column.shape[0]
    capacity = max(2, 4 * obs_total // tiles)
    share = channels // levs

    tables = jnp.stack([static_scales, local_scales])
    marks = (
        scale_class[None] == lax.broadcasted_iota(jnp.int32, (classes, lons, lats), 0)
    ).astype(jnp.float32)
    kappas = jnp.sum(tables[:, :, None, None] * marks[None], axis=1)

    source = obs_source[:, 0]
    source_marks = source[:, None] == lax.broadcasted_iota(jnp.int32, (obs_total, tiles), 1)
    earlier = (
        lax.broadcasted_iota(jnp.int32, (obs_total, obs_total), 1)
        < lax.broadcasted_iota(jnp.int32, (obs_total, obs_total), 0)
    ).astype(jnp.bfloat16)
    before = jnp.dot(earlier, source_marks.astype(jnp.bfloat16), preferred_element_type=jnp.float32)
    slot = jnp.sum(jnp.where(source_marks, before, 0.0), axis=1).astype(jnp.int32)
    place = source * capacity + slot
    place_marks = (
        place[:, None] == lax.broadcasted_iota(jnp.int32, (obs_total, tiles * capacity), 1)
    ).astype(jnp.float32)
    own_share = lambda value: lax.dynamic_slice_in_dim(value, lev_index * share, share, axis=0)
    payload = jnp.concatenate(
        [
            own_share(obs_weight),
            own_share(innovation),
            jnp.broadcast_to(obs_column.astype(jnp.float32)[None], (8, obs_total)),
        ],
        axis=0,
    )
    outgoing = jnp.dot(payload, place_marks, precision=highest)
    outgoing = outgoing.reshape(payload.shape[0], tiles, capacity).transpose(1, 0, 2)
    own_jac = obs_jac[0].reshape(channels, variables * levels)
    shape = lambda *dims: jax.ShapeDtypeStruct(dims, jnp.float32)
    own_rows, jacs, all_kappas, arrived = call(
        exchange_kernel, "exchange", 0,
        [shape(tiles, *band_sqrt.shape[1:]), shape(tiles, *own_jac.shape),
         shape(tiles, *kappas.shape), shape(*outgoing.shape)],
        [pltpu.SemaphoreType.DMA((4, tiles)), pltpu.SemaphoreType.DMA((4, tiles))],
        band_sqrt[0], own_jac, kappas, outgoing,
    )
    me = lax.axis_index("tile")
    beside = lambda step: lax.dynamic_index_in_dim(
        all_kappas, lax.rem(me + step + tiles, tiles), keepdims=False
    )
    wide_kappas = jnp.concatenate(
        [beside(-1)[:, -NSWEEP - 1:], kappas, beside(1)[:, :NSWEEP + 1]], axis=1
    )
    centre = wide_kappas[:, 1:-1]
    eastward = 0.5 * (centre + wide_kappas[:, 2:])
    westward = 0.5 * (wide_kappas[:, :-2] + centre)
    interior = 0.5 * (centre[:, :, :-1] + centre[:, :, 1:])
    edge_zero = jnp.zeros((2, centre.shape[1], 1), jnp.float32)
    northward = jnp.concatenate([interior, edge_zero], axis=2)
    southward = jnp.concatenate([edge_zero, interior], axis=2)
    inverse_diag = 1.0 / (1.0 + eastward + westward + northward + southward)
    weights = (eastward, westward, northward, southward, inverse_diag)
    wide_weights = jnp.stack(weights, axis=1)[:, :, :, None]
    wide_weights = jnp.broadcast_to(wide_weights, wide_weights.shape[:3] + (GROUP, lats))

    arrived = arrived.transpose(1, 0, 2).reshape(payload.shape[0], tiles * capacity)
    slots = tiles * capacity
    seen = arrived[2 * share].astype(jnp.int32)
    column_marks = (
        lax.broadcasted_iota(jnp.int32, (columns, slots), 0) == seen[None]
    ).astype(jnp.bfloat16)
    pair = lax.all_gather(arrived[:2 * share], "lev", axis=0, tiled=True)
    pair = pair.reshape(levs, 2, share, tiles, capacity).transpose(1, 3, 0, 2, 4)
    pair = pair.reshape(2, tiles, channels, capacity)
    slot_weight, slot_innovation = pair[0], pair[1]

    all_jacs = lax.all_gather(jacs, "lev", axis=2, tiled=True)

    own_rows = jnp.take(own_rows, band_owner, axis=0)
    roots = lax.all_gather(own_rows, "lev", axis=2, tiled=True)
    own_columns = lax.dynamic_slice_in_dim(roots, lev_index * levels, levels, axis=3)
    squares = jnp.einsum("bvlm,bvkm->bvlk", own_rows, roots, precision=highest)
    update = jnp.concatenate([own_columns.transpose(0, 1, 3, 2), squares], axis=2)
    update = update.transpose(1, 0, 2, 3).reshape(variables, -1, all_levels)

    def vertical(matrices, full):
        shaped = full.reshape(variables, all_levels, lons, bands, height)
        result = jnp.einsum("bvlm,vmxbr->vlxbr", matrices, shaped, precision=highest)
        return result.reshape(variables, matrices.shape[2], lons, lats)

    perts = ens_perts.transpose(0, 1, 3, 2, 4).astype(jnp.float32)

    fields = variables + members
    halo = pltpu.VMEM((fields, 2 * NSWEEP, levels, lats), jnp.float32)
    halo_sems = [pltpu.SemaphoreType.DMA((fields, 2))] * 2
    lev_sems = [pltpu.SemaphoreType.DMA((variables, 3))] * 2
    source = pltpu.VMEM((fields, lons, levels, lats), jnp.float32)
    block = (variables, lons, levels, lats)

    def increment(mixed, ensemble, spread):
        return call(
            functools.partial(forward_kernel, spread), "forward", 1 if spread else 2,
            shape(levs, *block) if spread else shape(*block),
            [halo] + halo_sems + lev_sems, mixed, ensemble, perts, wide_weights,
        )

    turned = lambda value: value.transpose(0, 2, 1, 3)
    static, ensemble = turned(control_static), turned(control_ens)
    mixed = vertical(own_rows, lax.all_gather(control_static, "lev", axis=1, tiled=True))
    mixed = turned(mixed)
    for iteration in range(ITERS):
        full = increment(mixed, ensemble, True).transpose(0, 1, 3, 2, 4)
        full = full.reshape(levs * variables * levels, columns)
        high, low = split2(full)
        picked = jnp.dot(jnp.concatenate([high, low], axis=0), column_marks,
                         preferred_element_type=jnp.float32)
        picked = (picked[:full.shape[0]] + picked[full.shape[0]:]).reshape(-1, tiles, capacity)
        observed = jnp.einsum("tcj,jto->tco", all_jacs, picked, precision=highest)
        weighted = slot_weight * (observed - slot_innovation)
        pulled = jnp.einsum("tcj,tco->jto", jacs, weighted, precision=highest)
        pulled = pulled.reshape(-1, slots)
        high, low = split2(pulled)
        gradient = lax.dot_general(
            jnp.concatenate([high, low], axis=0), column_marks, (((1,), (1,)), ((), ())),
            preferred_element_type=jnp.float32,
        )
        gradient = gradient[:pulled.shape[0]] + gradient[pulled.shape[0]:]
        gradient = turned(gradient.reshape(control_static.shape))
        full, ensemble = call(
            backward_kernel, "backward", 3, [shape(levs, *block), shape(members, *block[1:])],
            [source, halo] + halo_sems + lev_sems, gradient, ensemble, perts, wide_weights,
        )
        static, mixed = call(
            vertical_kernel, "vertical", None, [shape(*block), shape(*block)], [],
            full, update, static, mixed,
        )
    return tuple(turned(value) for value in (increment(mixed, ensemble, False), static, ensemble))


def solution(mesh):
    return jax.shard_map(
        on_device,
        mesh=mesh,
        in_specs=(
            P(None, "lev", "tile", None),
            P(None, "lev", "tile", None),
            P(None, None, "lev", "tile", None),
            P("tile", None, "lev", None),
            P(),
            P("tile", None),
            P(),
            P(),
            P("tile", None),
            P("tile"),
            P("tile", None, None, "lev"),
            P(None, "tile"),
            P(None, "tile"),
        ),
        out_specs=(
            P(None, "lev", "tile", None),
            P(None, "lev", "tile", None),
            P(None, "lev", "tile", None),
        ),
        check_vma=False,
    )
```

```python
import functools

import jax
import jax.numpy as jnp
from jax import lax
from jax.experimental import pallas as pl
from jax.experimental.pallas import tpu as pltpu
from jax.sharding import PartitionSpec as P

NSWEEP = 4
ITERS = 2

beta_static = 0.8
beta_ensemble = 0.6
step_length = 0.3
highest = lax.Precision.HIGHEST
MESH = pl.DeviceIdType.MESH
GROUP = 8
vmem = pl.BlockSpec(memory_space=pltpu.VMEM)


def split2(value):
    high = lax.reduce_precision(value, 8, 7)
    return high.astype(jnp.bfloat16), (value - high).astype(jnp.bfloat16)


def greet(peers):
    barrier = pltpu.get_barrier_semaphore()
    for peer in peers:
        pl.semaphore_signal(barrier, inc=1, device_id=peer, device_id_type=MESH)
    pl.semaphore_wait(barrier, len(peers))


def tile_peers():
    tiles, me = lax.axis_size("tile"), lax.axis_index("tile")
    return {"tile": lax.rem(me + tiles - 1, tiles)}, {"tile": lax.rem(me + 1, tiles)}


def lev_peers():
    me = lax.axis_index("lev")
    core = lax.rem(me, 2)
    return me, me + 1 - 2 * core, me + 2 - 4 * (me // 2)


def halo_copies(field, halo, index, send, recv):
    left, right = tile_peers()
    half, lons = NSWEEP, field.shape[0]
    copies = []
    for side, peer, start in ((1, left, 0), (0, right, lons - half)):
        copies.append(
            pltpu.make_async_remote_copy(
                src_ref=field.at[pl.ds(start, half)],
                dst_ref=halo.at[index, pl.ds(side * half, half)],
                send_sem=send.at[index, side],
                recv_sem=recv.at[index, side],
                device_id=peer,
                device_id_type=MESH,
            )
        )
    return copies


def spread_copies(full, var, send, recv):
    me, core_peer, chip_peer = lev_peers()
    plan = ((me, core_peer), (me, chip_peer), (chip_peer, core_peer))
    return [
        pltpu.make_async_remote_copy(
            src_ref=full.at[block, var],
            dst_ref=full.at[block, var],
            send_sem=send.at[var, kind],
            recv_sem=recv.at[var, kind],
            device_id={"lev": peer},
            device_id_type=MESH,
        )
        for kind, (block, peer) in enumerate(plan)
    ]


def neighbours(wide, weights):
    lats = wide.shape[2]
    inner = wide[1:-1]
    return (weights[0] * wide[2:] + weights[1] * wide[:-2]) + (
        weights[2] * pltpu.roll(inner, lats - 1, 2) + weights[3] * pltpu.roll(inner, 1, 2)
    )


def kind_weights(w_ref, kind):
    return lambda i, start, count: w_ref[kind, i, pl.ds(start, count)]


def over_rows(levels, body):
    def step(i, carry):
        body(pl.ds(pl.multiple_of(i * GROUP, GROUP), GROUP))
        return carry

    lax.fori_loop(0, levels // GROUP, step, 0)


def widened(field, halo, index, rows):
    half = NSWEEP
    return jnp.concatenate(
        [halo[index, :half, rows], field[:, rows], halo[index, half:, rows]], axis=0
    )


def forward_rows(source, weights):
    current = source
    for sweep in range(1, NSWEEP + 1):
        count = source.shape[0] - 2 * sweep
        here = [weights(i, sweep, count) for i in range(5)]
        current = here[4] * (source[sweep:sweep + count] + neighbours(current, here))
    return current


def backward_rows(source, weights):
    lons = source.shape[0] - 2 * NSWEEP
    total, carried = 0.0, source
    for sweep in range(NSWEEP):
        count = source.shape[0] - 2 * sweep
        scaled = weights(4, sweep, count) * carried
        inner = NSWEEP - sweep
        total = total + scaled[inner:inner + lons]
        carried = neighbours(scaled, [weights(i, sweep + 1, count - 2) for i in range(4)])
    return total + carried


def forward_kernel(spread, mixed, ensemble, perts, w_ref, out, halo, hsend, hrecv, lsend, lrecv):
    variables, _, levels, _ = mixed.shape
    members = ensemble.shape[0]
    me, core_peer, chip_peer = lev_peers()
    greet(tile_peers() + (({"lev": core_peer}, {"lev": chip_peer}) if spread else ()))
    copies = [halo_copies(mixed.at[v], halo, v, hsend, hrecv) for v in range(variables)]
    copies += [
        halo_copies(ensemble.at[e], halo, variables + e, hsend, hrecv) for e in range(members)
    ]
    order = [variables + e for e in range(members)] + list(range(variables))
    for field in order:
        for copy in copies[field]:
            copy.start()
    block = out.at[me] if spread else out
    plans = [spread_copies(out, v, lsend, lrecv) for v in range(variables)] if spread else []
    for field in order:
        for copy in copies[field]:
            copy.wait_recv()
        static = field < variables
        weights = kind_weights(w_ref, 0 if static else 1)
        own = mixed.at[field] if static else ensemble.at[field - variables]

        def body(rows):
            result = forward_rows(widened(own, halo, field, rows), weights)
            if static:
                block[field, :, rows] += beta_static * result
            else:
                result = beta_ensemble * result
                for v in range(variables):
                    term = perts[field - variables, v, :, rows] * result
                    if field > variables:
                        term = block[v, :, rows] + term
                    block[v, :, rows] = term

        over_rows(levels, body)
        if static and spread:
            plans[field][1].start()
            plans[field][0].start()
    if spread:
        finish_spread(plans)
    for pair in copies:
        for copy in pair:
            copy.wait_send()


def finish_spread(plans):
    for plan in plans:
        plan[1].wait_recv()
        plan[2].start()
    for plan in plans:
        plan[0].wait_recv()
        plan[2].wait_recv()
        for copy in plan:
            copy.wait_send()


def backward_kernel(
    gradient, ensemble, perts, w_ref, full, updated, source, halo, hsend, hrecv, lsend, lrecv
):
    variables, _, levels, _ = gradient.shape
    members = ensemble.shape[0]
    me, core_peer, chip_peer = lev_peers()
    greet(tile_peers() + ({"lev": core_peer}, {"lev": chip_peer}))

    def mix(rows):
        parts = [gradient[v, :, rows] for v in range(variables)]
        for v in range(variables):
            source[v, :, rows] = beta_static * parts[v]
        for e in range(members):
            total = perts[e, 0, :, rows] * parts[0]
            for v in range(1, variables):
                total = total + perts[e, v, :, rows] * parts[v]
            source[variables + e, :, rows] = beta_ensemble * total

    over_rows(levels, mix)
    copies = [
        halo_copies(source.at[f], halo, f, hsend, hrecv) for f in range(variables + members)
    ]
    for pair in copies:
        for copy in pair:
            copy.start()
    plans = [spread_copies(full, v, lsend, lrecv) for v in range(variables)]
    for field in range(variables + members):
        for copy in copies[field]:
            copy.wait_recv()
        static = field < variables
        weights = kind_weights(w_ref, 0 if static else 1)

        def body(rows):
            result = backward_rows(widened(source.at[field], halo, field, rows), weights)
            if static:
                full[me, field, :, rows] = result
            else:
                held = ensemble[field - variables, :, rows]
                updated[field - variables, :, rows] = held - step_length * (held + result)

        over_rows(levels, body)
        if static:
            plans[field][1].start()
            plans[field][0].start()
    finish_spread(plans)
    for pair in copies:
        for copy in pair:
            copy.wait_send()


def exchange_kernel(
    matrix, jacobian, kappa, payload, matrices, jacobians, kappas, arrived, send, recv
):
    tiles, me = lax.axis_size("tile"), lax.axis_index("tile")
    barrier = pltpu.get_barrier_semaphore()

    def signal(offset, carry):
        peer = lax.rem(me + offset, tiles)
        pl.semaphore_signal(barrier, inc=1, device_id={"tile": peer}, device_id_type=MESH)
        return carry

    lax.fori_loop(1, tiles, signal, 0)
    pl.semaphore_wait(barrier, tiles - 1)

    def copies(offset):
        peer = lax.rem(me + offset, tiles)
        pairs = (
            (matrix, matrices.at[me]),
            (jacobian, jacobians.at[me]),
            (kappa, kappas.at[me]),
            (payload.at[peer], arrived.at[me]),
        )
        return [
            pltpu.make_async_remote_copy(
                src_ref=src,
                dst_ref=dst,
                send_sem=send.at[k, offset],
                recv_sem=recv.at[k, offset],
                device_id={"tile": peer},
                device_id_type=MESH,
            )
            for k, (src, dst) in enumerate(pairs)
        ]

    def begin(offset, carry):
        for copy in copies(offset):
            copy.start()
        return carry

    lax.fori_loop(1, tiles, begin, 0)
    matrices[me] = matrix[...]
    jacobians[me] = jacobian[...]
    kappas[me] = kappa[...]
    arrived[me] = payload[me]

    def finish(offset, carry):
        for copy in copies(offset):
            copy.wait()
        return carry

    lax.fori_loop(1, tiles, finish, 0)


def vertical_kernel(full, matrices, static, mixed, new_static, new_mixed):
    levs, variables, lons, levels, lats = full.shape
    rows = 2 * levels
    bands = matrices.shape[1] // rows
    band = lax.broadcasted_iota(jnp.int32, (rows, lats), 1) // (lats // bands)

    def step(x, carry):
        for v in range(variables):
            column = jnp.concatenate([full[block, v, x] for block in range(levs)], axis=0)
            product = jnp.dot(
                matrices[v], column, precision=highest, preferred_element_type=jnp.float32
            )
            kept = product[:rows]
            for b in range(1, bands):
                kept = jnp.where(band == b, product[b * rows:(b + 1) * rows], kept)
            held, other = static[v, x], mixed[v, x]
            new_static[v, x] = held - step_length * (held + kept[:levels])
            new_mixed[v, x] = other - step_length * (other + kept[levels:])
        return carry

    lax.fori_loop(0, lons, step, 0)


def call(kernel, name, identity, shapes, scratch, *operands):
    many = isinstance(shapes, list)
    result = pl.pallas_call(
        kernel,
        name=name,
        out_shape=shapes if many else [shapes],
        in_specs=[vmem] * len(operands),
        out_specs=[vmem] * (len(shapes) if many else 1),
        scratch_shapes=scratch,
        compiler_params=pltpu.CompilerParams(
            collective_id=identity,
            has_side_effects=identity is not None,
            vmem_limit_bytes=40 * 2**20,
        ),
    )(*operands)
    return result if many else result[0]


def on_device(
    control_static,
    control_ens,
    ens_perts,
    band_sqrt,
    band_owner,
    scale_class,
    static_scales,
    local_scales,
    obs_source,
    obs_column,
    obs_jac,
    innovation,
    obs_weight,
):
    tiles = lax.axis_size("tile")
    levs = lax.axis_size("lev")
    lev_index = lax.axis_index("lev")
    variables, levels, lons, lats = control_static.shape
    members = control_ens.shape[0]
    all_levels = band_sqrt.shape[3]
    bands = band_owner.shape[0]
    height = lats // bands
    classes = static_scales.shape[0]
    columns = lons * lats
    channels = obs_jac.shape[1]
    obs_total = obs_column.shape[0]
    capacity = max(2, 4 * obs_total // tiles)
    share = channels // levs

    tables = jnp.stack([static_scales, local_scales])
    marks = (
        scale_class[None] == lax.broadcasted_iota(jnp.int32, (classes, lons, lats), 0)
    ).astype(jnp.float32)
    kappas = jnp.sum(tables[:, :, None, None] * marks[None], axis=1)

    source = obs_source[:, 0]
    source_marks = source[:, None] == lax.broadcasted_iota(jnp.int32, (obs_total, tiles), 1)
    earlier = (
        lax.broadcasted_iota(jnp.int32, (obs_total, obs_total), 1)
        < lax.broadcasted_iota(jnp.int32, (obs_total, obs_total), 0)
    ).astype(jnp.bfloat16)
    before = jnp.dot(earlier, source_marks.astype(jnp.bfloat16), preferred_element_type=jnp.float32)
    slot = jnp.sum(jnp.where(source_marks, before, 0.0), axis=1).astype(jnp.int32)
    place = source * capacity + slot
    place_marks = (
        place[:, None] == lax.broadcasted_iota(jnp.int32, (obs_total, tiles * capacity), 1)
    ).astype(jnp.float32)
    own_share = lambda value: lax.dynamic_slice_in_dim(value, lev_index * share, share, axis=0)
    payload = jnp.concatenate(
        [
            own_share(obs_weight),
            own_share(innovation),
            jnp.broadcast_to(obs_column.astype(jnp.float32)[None], (8, obs_total)),
        ],
        axis=0,
    )
    outgoing = jnp.dot(payload, place_marks, precision=highest)
    outgoing = outgoing.reshape(payload.shape[0], tiles, capacity).transpose(1, 0, 2)
    own_jac = obs_jac[0].reshape(channels, variables * levels)
    shape = lambda *dims: jax.ShapeDtypeStruct(dims, jnp.float32)
    own_rows, jacs, all_kappas, arrived = call(
        exchange_kernel, "exchange", 0,
        [shape(tiles, *band_sqrt.shape[1:]), shape(tiles, *own_jac.shape),
         shape(tiles, *kappas.shape), shape(*outgoing.shape)],
        [pltpu.SemaphoreType.DMA((4, tiles)), pltpu.SemaphoreType.DMA((4, tiles))],
        band_sqrt[0], own_jac, kappas, outgoing,
    )
    me = lax.axis_index("tile")
    beside = lambda step: lax.dynamic_index_in_dim(
        all_kappas, lax.rem(me + step + tiles, tiles), keepdims=False
    )
    wide_kappas = jnp.concatenate(
        [beside(-1)[:, -NSWEEP - 1:], kappas, beside(1)[:, :NSWEEP + 1]], axis=1
    )
    centre = wide_kappas[:, 1:-1]
    eastward = 0.5 * (centre + wide_kappas[:, 2:])
    westward = 0.5 * (wide_kappas[:, :-2] + centre)
    interior = 0.5 * (centre[:, :, :-1] + centre[:, :, 1:])
    edge_zero = jnp.zeros((2, centre.shape[1], 1), jnp.float32)
    northward = jnp.concatenate([interior, edge_zero], axis=2)
    southward = jnp.concatenate([edge_zero, interior], axis=2)
    inverse_diag = 1.0 / (1.0 + eastward + westward + northward + southward)
    weights = (eastward, westward, northward, southward, inverse_diag)
    wide_weights = jnp.stack(weights, axis=1)[:, :, :, None]
    wide_weights = jnp.broadcast_to(wide_weights, wide_weights.shape[:3] + (GROUP, lats))

    arrived = arrived.transpose(1, 0, 2).reshape(payload.shape[0], tiles * capacity)
    slots = tiles * capacity
    seen = arrived[2 * share].astype(jnp.int32)
    column_marks = (
        lax.broadcasted_iota(jnp.int32, (columns, slots), 0) == seen[None]
    ).astype(jnp.bfloat16)
    pair = lax.all_gather(arrived[:2 * share], "lev", axis=0, tiled=True)
    pair = pair.reshape(levs, 2, share, tiles, capacity).transpose(1, 3, 0, 2, 4)
    pair = pair.reshape(2, tiles, channels, capacity)
    slot_weight, slot_innovation = pair[0], pair[1]

    all_jacs = lax.all_gather(jacs, "lev", axis=2, tiled=True)

    own_rows = jnp.take(own_rows, band_owner, axis=0)
    roots = lax.all_gather(own_rows, "lev", axis=2, tiled=True)

    def vertical(matrices, full):
        shaped = full.reshape(variables, all_levels, lons, bands, height)
        result = jnp.einsum("bvlm,vmxbr->vlxbr", matrices, shaped, precision=highest)
        return result.reshape(variables, matrices.shape[2], lons, lats)

    perts = ens_perts.transpose(0, 1, 3, 2, 4).astype(jnp.float32)

    fields = variables + members
    halo = pltpu.VMEM((fields, 2 * NSWEEP, levels, lats), jnp.float32)
    halo_sems = [pltpu.SemaphoreType.DMA((fields, 2))] * 2
    lev_sems = [pltpu.SemaphoreType.DMA((variables, 3))] * 2
    source = pltpu.VMEM((fields, lons, levels, lats), jnp.float32)
    block = (variables, lons, levels, lats)

    def increment(mixed, ensemble, spread):
        return call(
            functools.partial(forward_kernel, spread), "forward", 1 if spread else 2,
            shape(levs, *block) if spread else shape(*block),
            [halo] + halo_sems + lev_sems, mixed, ensemble, perts, wide_weights,
        )

    turned = lambda value: value.transpose(0, 2, 1, 3)
    static, ensemble = turned(control_static), turned(control_ens)
    mixed = vertical(own_rows, lax.all_gather(control_static, "lev", axis=1, tiled=True))
    mixed = turned(mixed)
    for iteration in range(ITERS):
        full = increment(mixed, ensemble, True).transpose(0, 1, 3, 2, 4)
        full = full.reshape(levs * variables * levels, columns)
        high, low = split2(full)
        picked = jnp.dot(jnp.concatenate([high, low], axis=0), column_marks,
                         preferred_element_type=jnp.float32)
        picked = (picked[:full.shape[0]] + picked[full.shape[0]:]).reshape(-1, tiles, capacity)
        observed = jnp.einsum("tcj,jto->tco", all_jacs, picked, precision=highest)
        weighted = slot_weight * (observed - slot_innovation)
        pulled = jnp.einsum("tcj,tco->jto", jacs, weighted, precision=highest)
        pulled = pulled.reshape(-1, slots)
        high, low = split2(pulled)
        gradient = lax.dot_general(
            jnp.concatenate([high, low], axis=0), column_marks, (((1,), (1,)), ((), ())),
            preferred_element_type=jnp.float32,
        )
        gradient = gradient[:pulled.shape[0]] + gradient[pulled.shape[0]:]
        gradient = turned(gradient.reshape(control_static.shape))
        full, ensemble = call(
            backward_kernel, "backward", 3, [shape(levs, *block), shape(members, *block[1:])],
            [source, halo] + halo_sems + lev_sems, gradient, ensemble, perts, wide_weights,
        )
        if iteration == 0:
            roots, full = lax.optimization_barrier((roots, full))
            own_columns = lax.dynamic_slice_in_dim(roots, lev_index * levels, levels, axis=3)
            squares = jnp.einsum("bvlm,bvkm->bvlk", own_rows, roots, precision=highest)
            update = jnp.concatenate([own_columns.transpose(0, 1, 3, 2), squares], axis=2)
            update = update.transpose(1, 0, 2, 3).reshape(variables, -1, all_levels)
        static, mixed = call(
            vertical_kernel, "vertical", None, [shape(*block), shape(*block)], [],
            full, update, static, mixed,
        )
    return tuple(turned(value) for value in (increment(mixed, ensemble, False), static, ensemble))


def solution(mesh):
    return jax.shard_map(
        on_device,
        mesh=mesh,
        in_specs=(
            P(None, "lev", "tile", None),
            P(None, "lev", "tile", None),
            P(None, None, "lev", "tile", None),
            P("tile", None, "lev", None),
            P(),
            P("tile", None),
            P(),
            P(),
            P("tile", None),
            P("tile"),
            P("tile", None, None, "lev"),
            P(None, "tile"),
            P(None, "tile"),
        ),
        out_specs=(
            P(None, "lev", "tile", None),
            P(None, "lev", "tile", None),
            P(None, "lev", "tile", None),
        ),
        check_vma=False,
    )
```

```python
import functools

import jax
import jax.numpy as jnp
from jax import lax
from jax.experimental import pallas as pl
from jax.experimental.pallas import tpu as pltpu
from jax.sharding import PartitionSpec as P

NSWEEP = 4
ITERS = 2

beta_static = 0.8
beta_ensemble = 0.6
step_length = 0.3
highest = lax.Precision.HIGHEST
MESH = pl.DeviceIdType.MESH
GROUP = 8
vmem = pl.BlockSpec(memory_space=pltpu.VMEM)


def split2(value):
    high = lax.reduce_precision(value, 8, 7)
    return high.astype(jnp.bfloat16), (value - high).astype(jnp.bfloat16)


def greet(peers):
    barrier = pltpu.get_barrier_semaphore()
    for peer in peers:
        pl.semaphore_signal(barrier, inc=1, device_id=peer, device_id_type=MESH)
    pl.semaphore_wait(barrier, len(peers))


def tile_peers():
    tiles, me = lax.axis_size("tile"), lax.axis_index("tile")
    return {"tile": lax.rem(me + tiles - 1, tiles)}, {"tile": lax.rem(me + 1, tiles)}


def lev_peers():
    me = lax.axis_index("lev")
    core = lax.rem(me, 2)
    return me, me + 1 - 2 * core, me + 2 - 4 * (me // 2)


def halo_copies(field, halo, index, send, recv):
    left, right = tile_peers()
    half, lons = NSWEEP, field.shape[0]
    copies = []
    for side, peer, start in ((1, left, 0), (0, right, lons - half)):
        copies.append(
            pltpu.make_async_remote_copy(
                src_ref=field.at[pl.ds(start, half)],
                dst_ref=halo.at[index, pl.ds(side * half, half)],
                send_sem=send.at[index, side],
                recv_sem=recv.at[index, side],
                device_id=peer,
                device_id_type=MESH,
            )
        )
    return copies


def spread_copies(full, var, send, recv):
    me, core_peer, chip_peer = lev_peers()
    plan = ((me, core_peer), (me, chip_peer), (chip_peer, core_peer))
    return [
        pltpu.make_async_remote_copy(
            src_ref=full.at[block, var],
            dst_ref=full.at[block, var],
            send_sem=send.at[var, kind],
            recv_sem=recv.at[var, kind],
            device_id={"lev": peer},
            device_id_type=MESH,
        )
        for kind, (block, peer) in enumerate(plan)
    ]


def neighbours(wide, weights):
    lats = wide.shape[2]
    inner = wide[1:-1]
    return (weights[0] * wide[2:] + weights[1] * wide[:-2]) + (
        weights[2] * pltpu.roll(inner, lats - 1, 2) + weights[3] * pltpu.roll(inner, 1, 2)
    )


def kind_weights(w_ref, kind):
    return lambda i, start, count: w_ref[kind, i, pl.ds(start, count)]


def over_rows(levels, body):
    def step(i, carry):
        body(pl.ds(pl.multiple_of(i * GROUP, GROUP), GROUP))
        return carry

    lax.fori_loop(0, levels // GROUP, step, 0)


def widened(field, halo, index, rows):
    half = NSWEEP
    return jnp.concatenate(
        [halo[index, :half, rows], field[:, rows], halo[index, half:, rows]], axis=0
    )


def forward_rows(source, weights):
    current = source
    for sweep in range(1, NSWEEP + 1):
        count = source.shape[0] - 2 * sweep
        here = [weights(i, sweep, count) for i in range(5)]
        current = here[4] * (source[sweep:sweep + count] + neighbours(current, here))
    return current


def backward_rows(source, weights):
    lons = source.shape[0] - 2 * NSWEEP
    total, carried = 0.0, source
    for sweep in range(NSWEEP):
        count = source.shape[0] - 2 * sweep
        scaled = weights(4, sweep, count) * carried
        inner = NSWEEP - sweep
        total = total + scaled[inner:inner + lons]
        carried = neighbours(scaled, [weights(i, sweep + 1, count - 2) for i in range(4)])
    return total + carried


def forward_kernel(spread, mixed, ensemble, perts, w_ref, out, halo, hsend, hrecv, lsend, lrecv):
    variables, _, levels, _ = mixed.shape
    members = ensemble.shape[0]
    me, core_peer, chip_peer = lev_peers()
    greet(tile_peers() + (({"lev": core_peer}, {"lev": chip_peer}) if spread else ()))
    copies = [halo_copies(mixed.at[v], halo, v, hsend, hrecv) for v in range(variables)]
    copies += [
        halo_copies(ensemble.at[e], halo, variables + e, hsend, hrecv) for e in range(members)
    ]
    order = [variables + e for e in range(members)] + list(range(variables))
    for field in order:
        for copy in copies[field]:
            copy.start()
    block = out.at[me] if spread else out
    plans = [spread_copies(out, v, lsend, lrecv) for v in range(variables)] if spread else []
    for field in order:
        for copy in copies[field]:
            copy.wait_recv()
        static = field < variables
        weights = kind_weights(w_ref, 0 if static else 1)
        own = mixed.at[field] if static else ensemble.at[field - variables]

        def body(rows):
            result = forward_rows(widened(own, halo, field, rows), weights)
            if static:
                block[field, :, rows] += beta_static * result
            else:
                result = beta_ensemble * result
                for v in range(variables):
                    term = perts[field - variables, v, :, rows] * result
                    if field > variables:
                        term = block[v, :, rows] + term
                    block[v, :, rows] = term

        over_rows(levels, body)
        if static and spread:
            plans[field][1].start()
            plans[field][0].start()
    if spread:
        finish_spread(plans)
    for pair in copies:
        for copy in pair:
            copy.wait_send()


def finish_spread(plans):
    for plan in plans:
        plan[1].wait_recv()
        plan[2].start()
    for plan in plans:
        plan[0].wait_recv()
        plan[2].wait_recv()
        for copy in plan:
            copy.wait_send()


def backward_kernel(
    gradient, ensemble, perts, w_ref, full, updated, source, halo, hsend, hrecv, lsend, lrecv
):
    variables, _, levels, _ = gradient.shape
    members = ensemble.shape[0]
    me, core_peer, chip_peer = lev_peers()
    greet(tile_peers() + ({"lev": core_peer}, {"lev": chip_peer}))

    def mix(rows):
        parts = [gradient[v, :, rows] for v in range(variables)]
        for v in range(variables):
            source[v, :, rows] = beta_static * parts[v]
        for e in range(members):
            total = perts[e, 0, :, rows] * parts[0]
            for v in range(1, variables):
                total = total + perts[e, v, :, rows] * parts[v]
            source[variables + e, :, rows] = beta_ensemble * total

    over_rows(levels, mix)
    copies = [
        halo_copies(source.at[f], halo, f, hsend, hrecv) for f in range(variables + members)
    ]
    for pair in copies:
        for copy in pair:
            copy.start()
    plans = [spread_copies(full, v, lsend, lrecv) for v in range(variables)]
    for field in range(variables + members):
        for copy in copies[field]:
            copy.wait_recv()
        static = field < variables
        weights = kind_weights(w_ref, 0 if static else 1)

        def body(rows):
            result = backward_rows(widened(source.at[field], halo, field, rows), weights)
            if static:
                full[me, field, :, rows] = result
            else:
                held = ensemble[field - variables, :, rows]
                updated[field - variables, :, rows] = held - step_length * (held + result)

        over_rows(levels, body)
        if static:
            plans[field][1].start()
            plans[field][0].start()
    finish_spread(plans)
    for pair in copies:
        for copy in pair:
            copy.wait_send()


def exchange_kernel(
    matrix, jacobian, kappa, payload, matrices, jacobians, kappas, arrived, send, recv
):
    tiles, me = lax.axis_size("tile"), lax.axis_index("tile")
    barrier = pltpu.get_barrier_semaphore()

    def signal(offset, carry):
        peer = lax.rem(me + offset, tiles)
        pl.semaphore_signal(barrier, inc=1, device_id={"tile": peer}, device_id_type=MESH)
        return carry

    lax.fori_loop(1, tiles, signal, 0)
    pl.semaphore_wait(barrier, tiles - 1)

    def copies(offset):
        peer = lax.rem(me + offset, tiles)
        pairs = (
            (matrix, matrices.at[me]),
            (jacobian, jacobians.at[me]),
            (kappa, kappas.at[me]),
            (payload.at[peer], arrived.at[me]),
        )
        return [
            pltpu.make_async_remote_copy(
                src_ref=src,
                dst_ref=dst,
                send_sem=send.at[k, offset],
                recv_sem=recv.at[k, offset],
                device_id={"tile": peer},
                device_id_type=MESH,
            )
            for k, (src, dst) in enumerate(pairs)
        ]

    def begin(offset, carry):
        for copy in copies(offset):
            copy.start()
        return carry

    lax.fori_loop(1, tiles, begin, 0)
    matrices[me] = matrix[...]
    jacobians[me] = jacobian[...]
    kappas[me] = kappa[...]
    arrived[me] = payload[me]

    def finish(offset, carry):
        for copy in copies(offset):
            copy.wait()
        return carry

    lax.fori_loop(1, tiles, finish, 0)


def vertical_kernel(full, matrices, static, mixed, new_static, new_mixed):
    levs, variables, lons, levels, lats = full.shape
    rows = 2 * levels
    bands = matrices.shape[1] // rows
    band = lax.broadcasted_iota(jnp.int32, (rows, lats), 1) // (lats // bands)

    def step(x, carry):
        for v in range(variables):
            column = jnp.concatenate([full[block, v, x] for block in range(levs)], axis=0)
            product = jnp.dot(
                matrices[v], column, precision=highest, preferred_element_type=jnp.float32
            )
            kept = product[:rows]
            for b in range(1, bands):
                kept = jnp.where(band == b, product[b * rows:(b + 1) * rows], kept)
            held, other = static[v, x], mixed[v, x]
            new_static[v, x] = held - step_length * (held + kept[:levels])
            new_mixed[v, x] = other - step_length * (other + kept[levels:])
        return carry

    lax.fori_loop(0, lons, step, 0)


def call(kernel, name, identity, shapes, scratch, *operands):
    many = isinstance(shapes, list)
    result = pl.pallas_call(
        kernel,
        name=name,
        out_shape=shapes if many else [shapes],
        in_specs=[vmem] * len(operands),
        out_specs=[vmem] * (len(shapes) if many else 1),
        scratch_shapes=scratch,
        compiler_params=pltpu.CompilerParams(
            collective_id=identity,
            has_side_effects=identity is not None,
            vmem_limit_bytes=40 * 2**20,
        ),
    )(*operands)
    return result if many else result[0]


def on_device(
    control_static,
    control_ens,
    ens_perts,
    band_sqrt,
    band_owner,
    scale_class,
    static_scales,
    local_scales,
    obs_source,
    obs_column,
    obs_jac,
    innovation,
    obs_weight,
):
    tiles = lax.axis_size("tile")
    levs = lax.axis_size("lev")
    lev_index = lax.axis_index("lev")
    variables, levels, lons, lats = control_static.shape
    members = control_ens.shape[0]
    all_levels = band_sqrt.shape[3]
    bands = band_owner.shape[0]
    height = lats // bands
    classes = static_scales.shape[0]
    columns = lons * lats
    channels = obs_jac.shape[1]
    obs_total = obs_column.shape[0]
    capacity = max(2, 4 * obs_total // tiles)
    share = channels // levs

    tables = jnp.stack([static_scales, local_scales])
    marks = (
        scale_class[None] == lax.broadcasted_iota(jnp.int32, (classes, lons, lats), 0)
    ).astype(jnp.float32)
    kappas = jnp.sum(tables[:, :, None, None] * marks[None], axis=1)

    source = obs_source[:, 0]
    source_marks = source[:, None] == lax.broadcasted_iota(jnp.int32, (obs_total, tiles), 1)
    earlier = (
        lax.broadcasted_iota(jnp.int32, (obs_total, obs_total), 1)
        < lax.broadcasted_iota(jnp.int32, (obs_total, obs_total), 0)
    ).astype(jnp.bfloat16)
    before = jnp.dot(earlier, source_marks.astype(jnp.bfloat16), preferred_element_type=jnp.float32)
    slot = jnp.sum(jnp.where(source_marks, before, 0.0), axis=1).astype(jnp.int32)
    place = source * capacity + slot
    place_marks = (
        place[:, None] == lax.broadcasted_iota(jnp.int32, (obs_total, tiles * capacity), 1)
    ).astype(jnp.float32)
    own_share = lambda value: lax.dynamic_slice_in_dim(value, lev_index * share, share, axis=0)
    payload = jnp.concatenate(
        [
            own_share(obs_weight),
            own_share(innovation),
            jnp.broadcast_to(obs_column.astype(jnp.float32)[None], (8, obs_total)),
        ],
        axis=0,
    )
    outgoing = jnp.dot(payload, place_marks, precision=highest)
    outgoing = outgoing.reshape(payload.shape[0], tiles, capacity).transpose(1, 0, 2)
    own_jac = obs_jac[0].reshape(channels, variables * levels)
    shape = lambda *dims: jax.ShapeDtypeStruct(dims, jnp.float32)
    own_rows, jacs, all_kappas, arrived = call(
        exchange_kernel, "exchange", 0,
        [shape(tiles, *band_sqrt.shape[1:]), shape(tiles, *own_jac.shape),
         shape(tiles, *kappas.shape), shape(*outgoing.shape)],
        [pltpu.SemaphoreType.DMA((4, tiles)), pltpu.SemaphoreType.DMA((4, tiles))],
        band_sqrt[0], own_jac, kappas, outgoing,
    )
    me = lax.axis_index("tile")
    beside = lambda step: lax.dynamic_index_in_dim(
        all_kappas, lax.rem(me + step + tiles, tiles), keepdims=False
    )
    wide_kappas = jnp.concatenate(
        [beside(-1)[:, -NSWEEP - 1:], kappas, beside(1)[:, :NSWEEP + 1]], axis=1
    )
    centre = wide_kappas[:, 1:-1]
    eastward = 0.5 * (centre + wide_kappas[:, 2:])
    westward = 0.5 * (wide_kappas[:, :-2] + centre)
    interior = 0.5 * (centre[:, :, :-1] + centre[:, :, 1:])
    edge_zero = jnp.zeros((2, centre.shape[1], 1), jnp.float32)
    northward = jnp.concatenate([interior, edge_zero], axis=2)
    southward = jnp.concatenate([edge_zero, interior], axis=2)
    inverse_diag = 1.0 / (1.0 + eastward + westward + northward + southward)
    weights = (eastward, westward, northward, southward, inverse_diag)
    wide_weights = jnp.stack(weights, axis=1)[:, :, :, None]
    wide_weights = jnp.broadcast_to(wide_weights, wide_weights.shape[:3] + (GROUP, lats))

    arrived = arrived.transpose(1, 0, 2).reshape(payload.shape[0], tiles * capacity)
    slots = tiles * capacity
    seen = arrived[2 * share].astype(jnp.int32)
    column_marks = (
        lax.broadcasted_iota(jnp.int32, (columns, slots), 0) == seen[None]
    ).astype(jnp.bfloat16)
    pair = lax.all_gather(arrived[:2 * share], "lev", axis=0, tiled=True)
    pair = pair.reshape(levs, 2, share, tiles, capacity).transpose(1, 3, 0, 2, 4)
    pair = pair.reshape(2, tiles, channels, capacity)
    slot_weight, slot_innovation = pair[0], pair[1]

    all_jacs = lax.all_gather(jacs, "lev", axis=2, tiled=True)

    own_rows = jnp.take(own_rows, band_owner, axis=0)
    roots = lax.all_gather(own_rows, "lev", axis=2, tiled=True)

    def vertical(matrices, full):
        shaped = full.reshape(variables, all_levels, lons, bands, height)
        result = jnp.einsum("bvlm,vmxbr->vlxbr", matrices, shaped, precision=highest)
        return result.reshape(variables, matrices.shape[2], lons, lats)

    perts = ens_perts.transpose(0, 1, 3, 2, 4).astype(jnp.float32)

    fields = variables + members
    halo = pltpu.VMEM((fields, 2 * NSWEEP, levels, lats), jnp.float32)
    halo_sems = [pltpu.SemaphoreType.DMA((fields, 2))] * 2
    lev_sems = [pltpu.SemaphoreType.DMA((variables, 3))] * 2
    source = pltpu.VMEM((fields, lons, levels, lats), jnp.float32)
    block = (variables, lons, levels, lats)

    def increment(mixed, ensemble, spread):
        return call(
            functools.partial(forward_kernel, spread), "forward", 1 if spread else 2,
            shape(levs, *block) if spread else shape(*block),
            [halo] + halo_sems + lev_sems, mixed, ensemble, perts, wide_weights,
        )

    turned = lambda value: value.transpose(0, 2, 1, 3)
    static, ensemble = turned(control_static), turned(control_ens)
    mixed = vertical(own_rows, lax.all_gather(control_static, "lev", axis=1, tiled=True))
    mixed = turned(mixed)
    for iteration in range(ITERS):
        full = increment(mixed, ensemble, True).transpose(0, 1, 3, 2, 4)
        full = full.reshape(levs * variables * levels, columns)
        high, low = split2(full)
        picked = jnp.dot(jnp.concatenate([high, low], axis=0), column_marks,
                         preferred_element_type=jnp.float32)
        picked = (picked[:full.shape[0]] + picked[full.shape[0]:]).reshape(-1, tiles, capacity)
        observed = jnp.einsum("tcj,jto->tco", all_jacs, picked, precision=lax.Precision.HIGH)
        weighted = slot_weight * (observed - slot_innovation)
        pulled = jnp.einsum("tcj,tco->jto", jacs, weighted, precision=lax.Precision.HIGH)
        pulled = pulled.reshape(-1, slots)
        high, low = split2(pulled)
        gradient = lax.dot_general(
            jnp.concatenate([high, low], axis=0), column_marks, (((1,), (1,)), ((), ())),
            preferred_element_type=jnp.float32,
        )
        gradient = gradient[:pulled.shape[0]] + gradient[pulled.shape[0]:]
        gradient = turned(gradient.reshape(control_static.shape))
        full, ensemble = call(
            backward_kernel, "backward", 3, [shape(levs, *block), shape(members, *block[1:])],
            [source, halo] + halo_sems + lev_sems, gradient, ensemble, perts, wide_weights,
        )
        if iteration == 0:
            roots, full = lax.optimization_barrier((roots, full))
            own_columns = lax.dynamic_slice_in_dim(roots, lev_index * levels, levels, axis=3)
            squares = jnp.einsum("bvlm,bvkm->bvlk", own_rows, roots, precision=highest)
            update = jnp.concatenate([own_columns.transpose(0, 1, 3, 2), squares], axis=2)
            update = update.transpose(1, 0, 2, 3).reshape(variables, -1, all_levels)
        static, mixed = call(
            vertical_kernel, "vertical", None, [shape(*block), shape(*block)], [],
            full, update, static, mixed,
        )
    return tuple(turned(value) for value in (increment(mixed, ensemble, False), static, ensemble))


def solution(mesh):
    return jax.shard_map(
        on_device,
        mesh=mesh,
        in_specs=(
            P(None, "lev", "tile", None),
            P(None, "lev", "tile", None),
            P(None, None, "lev", "tile", None),
            P("tile", None, "lev", None),
            P(),
            P("tile", None),
            P(),
            P(),
            P("tile", None),
            P("tile"),
            P("tile", None, None, "lev"),
            P(None, "tile"),
            P(None, "tile"),
        ),
        out_specs=(
            P(None, "lev", "tile", None),
            P(None, "lev", "tile", None),
            P(None, "lev", "tile", None),
        ),
        check_vma=False,
    )
```
